32 devices in a mesh: phi: 8 (over z, core), mom: 4 (over y, x).
Axes of the slice: x: 2, y: 2, z: 4, core: 2. Of those that a mesh axis runs over, the one named last changes fastest.
Arguments:
- spectra: float32 [32, 4, 16, 64, 256], P('mom', None, 'phi'), may hold values from 0.1 to 3
- production: bfloat16 [32, 32], replicated, may hold values from 0 to 0.119628906
- bin_group: int32 [32], replicated, may hold values from 0 to 3
- parent_of: int32 [4], replicated, may hold values from 0 to 3
- diffusivity: float32 [64, 256], replicated, may hold values from 0.05 to 0.22
- height_inverse: float32 [64, 64], replicated, may hold values from -1 to 1, as said below
- loss_rate: float32 [32], P('mom'), may hold values from 2 to 20
- density: float32 [16, 64, 256], P('phi'), may hold values from 0.5 to 2
Outputs:
- spectra_out: float32 [32, 4, 16, 64, 256], P('mom', None, 'phi')
The draws below stay inside these ranges and needn't reach their ends.
Inputs may be any that keep to these rules, and one draw needn't show every extreme that they name: `height_inverse`: diagonal entries lie between 0.7 and 1, off-diagonal entries are small.
All inputs are finite; a program needn't handle non-finite values.
Results may differ from the reference program's by a relative error of at most 0.00085.
Values may be sent and summed in bfloat16 or wider, within the bound.
A program may use at most 64 MiB of HBM per device.

```python
import math
import jax
import jax.numpy as jnp
from jax import lax

P_SIZE = 32
S = 4
Z = 64
R = 256
STEPS = 1
NPHI = 16


def draw_height_inverse(key, part):
    first, second = jax.random.split(jax.random.fold_in(key, 17))
    diagonal = jax.random.uniform(first, (Z,), jnp.float32, 0.7, 1.0)
    spread = jnp.clip(jax.random.normal(second, (Z, Z), jnp.float32), -4.0, 4.0)
    eye_mask = jnp.eye(Z, dtype=jnp.float32)
    off_part = spread * (0.1 / jnp.sqrt(jnp.float32(Z))) * (1.0 - eye_mask)
    return eye_mask * diagonal[None, :] + off_part


def with_ends(values, own_key, low, top_value):
    extent = values.shape
    index_at = [jax.random.randint(jax.random.fold_in(own_key, axis), (), 0, extent[axis]) for axis in range(len(extent))]
    values = values.at[tuple(index_at)].set(low)
    longest = extent.index(max(extent))
    index_at[longest] = (index_at[longest] + 1) % extent[longest]
    return values.at[tuple(index_at)].set(top_value)


def block_levels(key, dims, cuts, low, high):
    def one(position, blocks):
        steps = jax.random.uniform(jax.random.fold_in(jax.random.fold_in(key, 6), position), (blocks,), jnp.float32, low / len(cuts), high / len(cuts))
        return jnp.repeat(jnp.exp(steps), dims[position] // blocks).reshape((-1,) + (1,) * (len(dims) - position - 1))

    loudness = one(*cuts[0])
    for cut in cuts[1:]:
        loudness = loudness * one(*cut)
    return loudness


def setup_inputs(seed: int = 0) -> dict:
    seeds = jax.random.split(jax.random.key(seed), 9)
    return {
        "spectra": jnp.clip(jnp.exp(math.log(3.0) - 3.4011974 * jax.random.uniform(seeds[0], (P_SIZE, S, NPHI, Z, R), jnp.float32) ** block_levels(seeds[0], (P_SIZE, S, NPHI, Z, R), ((0, 4), (2, 8)), -0.2, 0.2)), 0.1, 3.0),
        "production": jnp.clip(jax.random.uniform(seeds[1], (P_SIZE, P_SIZE), jnp.float32, 0.0, 0.119628906), 0.0, 0.119628906).astype(jnp.bfloat16),
        "bin_group": with_ends(jax.random.randint(seeds[2], (P_SIZE,), 0, 4), jax.random.fold_in(seeds[2], 1), 0, 3).astype(jnp.int32),
        "parent_of": with_ends(jax.random.randint(seeds[3], (S,), 0, S), jax.random.fold_in(seeds[3], 1), 0, S - 1).astype(jnp.int32),
        "diffusivity": jnp.clip(jnp.exp(jax.random.uniform(seeds[4], (Z, R), jnp.float32, math.log(0.05), math.log(0.22))), 0.05, 0.22),
        "height_inverse": draw_height_inverse(jax.random.fold_in(seeds[8], 71), 0),
        "loss_rate": jnp.clip(jnp.exp(math.log(20.0) - 2.3025851 * jax.random.uniform(seeds[6], (P_SIZE,), jnp.float32) ** block_levels(seeds[6], (P_SIZE,), ((0, 4),), -0.2, 0.2)), 2.0, 20.0),
        "density": jnp.clip(0.5 + 1.5 * jax.random.uniform(seeds[7], (NPHI, Z, R), jnp.float32) ** block_levels(seeds[7], (NPHI, Z, R), ((0, 8),), -0.2, 0.2), 0.5, 2.0),
    }


def one_step(state, production, bin_group, parent_of, diffusivity, height_inverse, loss_rate, density):
    onehot = (parent_of[:, None] == jnp.arange(S, dtype=jnp.int32)[None, :]).astype(jnp.float32)
    parents = jnp.einsum('st,qtxzr->qsxzr', onehot, state, precision=lax.Precision.HIGHEST).astype(jnp.bfloat16)
    same = bin_group[:, None] == bin_group[None, :]
    kernel = jnp.where(same, production, jnp.zeros_like(production))
    source = jnp.einsum('pq,qsxzr->psxzr', kernel.astype(jnp.float32), parents.astype(jnp.float32), precision=lax.Precision.HIGHEST)
    sourced = state + source
    lap_phi = jnp.roll(sourced, 1, axis=2) + jnp.roll(sourced, -1, axis=2) - 2.0 * sourced
    pad_r = jnp.pad(sourced, ((0, 0), (0, 0), (0, 0), (0, 0), (1, 1)))
    lap_r = pad_r[..., 2:] + pad_r[..., :-2] - 2.0 * sourced
    moved = sourced + diffusivity * lap_phi + 0.5 * diffusivity * lap_r
    pad_z = jnp.pad(moved, ((0, 0), (0, 0), (0, 0), (1, 1), (0, 0)))
    halfway = moved + 0.25 * (pad_z[:, :, :, 2:] + pad_z[:, :, :, :-2] - 2.0 * moved)
    settled = jnp.einsum('yz,psxzr->psxyr', height_inverse, halfway, precision=lax.Precision.HIGHEST)
    loss_coef = loss_rate[:, None, None, None, None] * density[None, None]
    coef_next = jnp.concatenate([loss_coef[1:], jnp.zeros_like(loss_coef[:1])], axis=0)
    settled_next = jnp.concatenate([settled[1:], jnp.zeros_like(settled[:1])], axis=0)
    right_side = (1.0 - 0.5 * loss_coef) * settled + 0.5 * coef_next * settled_next

    def downward(carry, inputs):
        right, coef, coef_up = inputs
        value = (right + 0.5 * coef_up * carry) / (1.0 + 0.5 * coef)
        return value, value

    start = jnp.zeros(settled.shape[1:], jnp.float32)
    unused, result = lax.scan(downward, start, (right_side, loss_coef, coef_next), reverse=True)
    return result


def reference(spectra, production, bin_group, parent_of, diffusivity, height_inverse, loss_rate, density):
    state = spectra
    for count in range(STEPS):
        state = one_step(state, production, bin_group, parent_of, diffusivity, height_inverse, loss_rate, density)
    return state
```

```python
import functools
import math

import jax
import jax.numpy as jnp
from jax import lax
from jax.experimental import pallas as pl
from jax.experimental.pallas import tpu as pltpu
from jax.sharding import PartitionSpec as P

MESH = pl.DeviceIdType.MESH
ROWS = 16


def grid_of(count):
    columns = max(d for d in range(1, math.isqrt(count) + 1) if count % d == 0)
    return count // columns, columns


def dot(a, b):
    return jnp.dot(a, b, preferred_element_type=jnp.float32)


def dot_nt(a, b):
    return lax.dot_general(a, b, (((1,), (1,)), ((), ())), preferred_element_type=jnp.float32)


def onehot_bins(first_bins, bins, total):
    local = lax.broadcasted_iota(jnp.int32, (bins, ROWS, total), 0)
    whole = lax.broadcasted_iota(jnp.int32, (bins, ROWS, total), 2)
    parts = [
        jnp.where(local + first == whole, 1.0, 0.0).reshape(bins * ROWS, total)
        for first in first_bins
    ]
    return jnp.concatenate(parts, axis=0).astype(jnp.bfloat16)


def step_kernel(
    ny,
    nx,
    f_ref,
    kernel_ref,
    parent_ref,
    diff_ref,
    inverse_ref,
    rate_ref,
    density_ref,
    out_ref,
    comb,
    ysend,
    yrecv,
    acc,
    faces_out,
    faces_in,
    hin,
    hout,
    weight,
    wide,
    height,
    coef,
    x_send,
    x_recv,
    y_send,
    y_recv,
    f_send,
    f_recv,
    h_send,
    h_recv,
):
    bins, species, cells, heights, radii = f_ref.shape
    total_bins = kernel_ref.shape[0]
    count = ny * nx
    chunks = species * cells
    phi = lax.axis_index("phi")
    mom = lax.axis_index("mom")
    phis = lax.axis_size("phi")
    row, col = mom // nx, mom % nx
    right, left = (phi + 1) % phis, (phi + phis - 1) % phis

    barrier = pltpu.get_barrier_semaphore()
    for d in range(1, count):
        pl.semaphore_signal(
            barrier, inc=1, device_id={"mom": (mom + d) % count}, device_id_type=MESH
        )
    for side in (left, right):
        pl.semaphore_signal(barrier, inc=1, device_id={"phi": side}, device_id_type=MESH)

    def x_copy(c, d):
        return pltpu.make_async_remote_copy(
            src_ref=comb.at[c, 0],
            dst_ref=comb.at[c, d],
            send_sem=x_send.at[c, d - 1],
            recv_sem=x_recv.at[c, d - 1],
            device_id={"mom": row * nx + (col + d) % nx},
            device_id_type=MESH,
        )

    def y_copy(c, e):
        return pltpu.make_async_remote_copy(
            src_ref=ysend.at[c, e - 1],
            dst_ref=yrecv.at[c, e - 1],
            send_sem=y_send.at[c, e - 1],
            recv_sem=y_recv.at[c, e - 1],
            device_id={"mom": ((row + e) % ny) * nx + col},
            device_id_type=MESH,
        )

    def face_copy(s, side):
        return pltpu.make_async_remote_copy(
            src_ref=faces_out.at[s, side],
            dst_ref=faces_in.at[s, side],
            send_sem=f_send.at[s, side],
            recv_sem=f_recv.at[s, side],
            device_id={"phi": left if side == 0 else right},
            device_id_type=MESH,
        )

    def h_copy(s):
        return pltpu.make_async_remote_copy(
            src_ref=hout.at[s],
            dst_ref=hin.at[s],
            send_sem=h_send.at[s],
            recv_sem=h_recv.at[s],
            device_id={"mom": (mom + count - 1) % count},
            device_id_type=MESH,
        )

    def fill_parents(s):
        parent = parent_ref[s]
        for x in range(cells):
            for q in range(bins):
                comb[s * cells + x, 0, q] = f_ref[q, parent, x].astype(jnp.bfloat16)

    def send_parents(s):
        for x in range(cells):
            for d in range(1, nx):
                x_copy(s * cells + x, d).start()

    fill_parents(0)
    pl.semaphore_wait(barrier, count + 1)
    send_parents(0)

    @pl.loop(1, species)
    def _(s):
        fill_parents(s)
        send_parents(s)

    rows_1h = onehot_bins([(((row + e) % ny) * nx + col) * bins for e in range(ny)], bins, total_bins)
    cols_1h = onehot_bins(
        [(row * nx + (col + nx - d) % nx) * bins for d in range(nx)], bins, total_bins
    )
    mixed = dot_nt(dot(rows_1h, kernel_ref[...]).astype(jnp.bfloat16), cols_1h)
    r_at = lax.broadcasted_iota(jnp.int32, mixed.shape, 0) & (ROWS - 1)
    c_at = lax.broadcasted_iota(jnp.int32, mixed.shape, 1) & (ROWS - 1)
    wide[...] = jnp.where(r_at == c_at, mixed, 0.0).astype(jnp.bfloat16)

    group = height.shape[1] // heights
    a_at = lax.broadcasted_iota(jnp.int32, (heights, heights), 0)
    b_at = lax.broadcasted_iota(jnp.int32, (heights, heights), 1)
    stencil = jnp.where(a_at == b_at, 0.5, 0.0) + jnp.where(jnp.abs(a_at - b_at) == 1, 0.25, 0.0)
    both = jnp.dot(
        inverse_ref[...],
        stencil,
        precision=lax.Precision.HIGHEST,
        preferred_element_type=jnp.float32,
    )
    high = both.astype(jnp.bfloat16).astype(jnp.float32)
    tall_a = lax.broadcasted_iota(jnp.int32, (group, heights, heights), 1)
    tall_b = lax.broadcasted_iota(jnp.int32, (group, heights, heights), 2)
    spread = jnp.where(tall_a == tall_b, 1.0, 0.0).reshape(group * heights, heights)
    spread = spread.astype(jnp.bfloat16)
    row_g = lax.broadcasted_iota(jnp.int32, (group, heights, group * heights), 0)
    col_g = lax.broadcasted_iota(jnp.int32, (group, heights, group * heights), 2)
    first = row_g * heights
    inside = jnp.where((col_g >= first) & (col_g < first + heights), 1.0, 0.0)
    inside = inside.reshape(group * heights, group * heights)
    for k, part in enumerate((high, both - high)):
        tall = jnp.concatenate([part] * group, axis=0).astype(jnp.bfloat16)
        height[k] = (dot_nt(tall, spread) * inside).astype(jnp.bfloat16)

    diff = diff_ref[...]
    lane = lax.broadcasted_iota(jnp.int32, diff.shape, 1)
    coef[0] = 1.0 - 3.0 * diff
    coef[1] = jnp.where(lane == 0, 0.0, 0.5 * diff)
    coef[2] = jnp.where(lane == radii - 1, 0.0, 0.5 * diff)

    for p in range(bins):
        half_rate = 0.5 * rate_ref[p]
        for x in range(cells):
            weight[p, x] = 1.0 / (1.0 + half_rate * density_ref[x])

    @pl.when(mom == count - 1)
    def _():
        hin[...] = jnp.zeros_like(hin)

    def mix(s):
        for x in range(cells):
            c = s * cells + x
            for d in range(1, nx):
                x_copy(c, d).wait_recv()

            @pl.loop(0, heights // ROWS)
            def _(k):
                at = pl.ds(pl.multiple_of(k * ROWS, ROWS), ROWS)
                block = comb[c, :, :, at, :].reshape(nx * bins * ROWS, radii)
                sums = dot(wide[...], block).reshape(ny, bins, ROWS, radii)
                acc[c, :, at, :] = f_ref[:, s, x, at, :] + sums[0]
                for e in range(1, ny):
                    ysend[c, e - 1, :, at, :] = sums[e].astype(jnp.bfloat16)

            for e in range(1, ny):
                y_copy(c, e).start()

    def source(s):
        for x in range(cells):
            c = s * cells + x
            for e in range(1, ny):
                y_copy(c, e).wait_recv()

            @pl.loop(0, bins)
            def _(p):
                value = acc[c, p]
                for e in range(1, ny):
                    value = value + yrecv[c, e - 1, p].astype(jnp.float32)
                acc[c, p] = value
                rounded = value.astype(jnp.bfloat16)
                if x == 0:
                    faces_out[s, 0, p] = rounded
                if x == cells - 1:
                    faces_out[s, 1, p] = rounded

            if x == 0:
                face_copy(s, 0).start()
            if x == cells - 1:
                face_copy(s, 1).start()

    def diffuse(s):
        face_copy(s, 0).wait_recv()
        face_copy(s, 1).wait_recv()
        first = s * cells
        per = group // cells

        @pl.loop(0, bins // per)
        def _(k):
            planes = []
            for j in range(per):
                p = k * per + j
                own = [acc[first + x, p] for x in range(cells)]
                before = [faces_in[s, 1, p].astype(jnp.float32)] + own[:-1]
                after = own[1:] + [faces_in[s, 0, p].astype(jnp.float32)]
                for x in range(cells):
                    moved = coef[0] * own[x] + diff_ref[...] * (before[x] + after[x])
                    moved += coef[1] * pltpu.roll(own[x], 1, 1)
                    moved += coef[2] * pltpu.roll(own[x], radii - 1, 1)
                    planes.append(moved)
            moved = jnp.concatenate(planes, axis=0)
            high = moved.astype(jnp.bfloat16)
            low = (moved - high.astype(jnp.float32)).astype(jnp.bfloat16)
            settled = dot(height[0], high) + dot(height[0], low) + dot(height[1], high)
            for j in range(per):
                for x in range(cells):
                    n = j * cells + x
                    acc[first + x, k * per + j] = settled[n * heights : (n + 1) * heights]

    def solve(s):
        @pl.when(mom < count - 1)
        def _():
            h_copy(s).wait_recv()

        span = heights // 2
        for x in range(cells):
            @pl.loop(0, 2)
            def _(k):
                at = pl.ds(pl.multiple_of(k * span, span), span)
                carry = hin[s, x, at, :]
                for p in range(bins - 1, -1, -1):
                    settled = acc[s * cells + x, p, at, :]
                    total = 2.0 * settled + carry
                    both = total * weight[p, x, at, :]
                    out_ref[p, s, x, at, :] = both - settled
                    carry = total - both
                hout[s, x, at, :] = carry

        @pl.when(mom > 0)
        def _():
            h_copy(s).start()

    @pl.loop(0, species + 2 + count)
    def _(i):
        @pl.when(i < species)
        def _():
            mix(i)

        @pl.when((i >= 1) & (i < species + 1))
        def _():
            source(i - 1)

        @pl.when((i >= 2) & (i < species + 2))
        def _():
            diffuse(i - 2)

        s = i - 2 - (count - 1 - mom)

        @pl.when((s >= 0) & (s < species))
        def _():
            solve(s)

    @pl.loop(0, species)
    def _(s):
        for x in range(cells):
            for d in range(1, nx):
                x_copy(s * cells + x, d).wait_send()
            for e in range(1, ny):
                y_copy(s * cells + x, e).wait_send()
        face_copy(s, 0).wait_send()
        face_copy(s, 1).wait_send()

        @pl.when(mom > 0)
        def _():
            h_copy(s).wait_send()


def local(
    ny,
    nx,
    spectra,
    production,
    bin_group,
    parent_of,
    diffusivity,
    height_inverse,
    loss_rate,
    density,
):
    bins, species, cells, heights, radii = spectra.shape
    same = bin_group[:, None] == bin_group[None, :]
    kernel = jnp.where(same, production, jnp.zeros_like(production))
    chunks = species * cells
    block = (bins, heights, radii)
    group = cells * max(1, 256 // (heights * cells))
    dma = pltpu.SemaphoreType.DMA
    vmem = pl.BlockSpec(memory_space=pltpu.VMEM)
    smem = pl.BlockSpec(memory_space=pltpu.SMEM)
    return pl.pallas_call(
        functools.partial(step_kernel, ny, nx),
        out_shape=jax.ShapeDtypeStruct(spectra.shape, jnp.float32),
        in_specs=[vmem, vmem, smem, vmem, vmem, smem, vmem],
        out_specs=vmem,
        scratch_shapes=[
            pltpu.VMEM((chunks, nx) + block, jnp.bfloat16),
            pltpu.VMEM((chunks, max(ny - 1, 1)) + block, jnp.bfloat16),
            pltpu.VMEM((chunks, max(ny - 1, 1)) + block, jnp.bfloat16),
            pltpu.VMEM((chunks,) + block, jnp.float32),
            pltpu.VMEM((species, 2) + block, jnp.bfloat16),
            pltpu.VMEM((species, 2) + block, jnp.bfloat16),
            pltpu.VMEM((species, cells, heights, radii), jnp.float32),
            pltpu.VMEM((species, cells, heights, radii), jnp.float32),
            pltpu.VMEM((bins, cells, heights, radii), jnp.float32),
            pltpu.VMEM((ny * bins * ROWS, nx * bins * ROWS), jnp.bfloat16),
            pltpu.VMEM((2, group * heights, group * heights), jnp.bfloat16),
            pltpu.VMEM((3, heights, radii), jnp.float32),
            dma((chunks, max(nx - 1, 1))),
            dma((chunks, max(nx - 1, 1))),
            dma((chunks, max(ny - 1, 1))),
            dma((chunks, max(ny - 1, 1))),
            dma((species, 2)),
            dma((species, 2)),
            dma((species,)),
            dma((species,)),
        ],
        compiler_params=pltpu.CompilerParams(
            collective_id=0, has_side_effects=True, vmem_limit_bytes=56 * 1024 * 1024
        ),
    )(spectra, kernel, parent_of, diffusivity, height_inverse, loss_rate, density)


def solution(mesh):
    ny, nx = grid_of(mesh.shape["mom"])
    return jax.shard_map(
        functools.partial(local, ny, nx),
        mesh=mesh,
        in_specs=(
            P("mom", None, "phi", None, None),
            P(),
            P(),
            P(),
            P(),
            P(),
            P("mom"),
            P("phi", None, None),
        ),
        out_specs=P("mom", None, "phi", None, None),
        check_vma=False,
    )
```

```python
import functools
import math

import jax
import jax.numpy as jnp
from jax import lax
from jax.experimental import pallas as pl
from jax.experimental.pallas import tpu as pltpu
from jax.sharding import PartitionSpec as P

MESH = pl.DeviceIdType.MESH
ROWS = 16


def grid_of(count):
    columns = max(d for d in range(1, math.isqrt(count) + 1) if count % d == 0)
    return count // columns, columns


def dot(a, b):
    return jnp.dot(a, b, preferred_element_type=jnp.float32)


def dot_nt(a, b):
    return lax.dot_general(a, b, (((1,), (1,)), ((), ())), preferred_element_type=jnp.float32)


def onehot_bins(first_bins, bins, total):
    local = lax.broadcasted_iota(jnp.int32, (bins, ROWS, total), 0)
    whole = lax.broadcasted_iota(jnp.int32, (bins, ROWS, total), 2)
    parts = [
        jnp.where(local + first == whole, 1.0, 0.0).reshape(bins * ROWS, total)
        for first in first_bins
    ]
    return jnp.concatenate(parts, axis=0).astype(jnp.bfloat16)


def step_kernel(
    ny,
    nx,
    f_hbm,
    kernel_ref,
    parent_ref,
    diff_ref,
    inverse_ref,
    rate_ref,
    density_ref,
    settled_ref,
    hin,
    f_ref,
    comb,
    psend,
    precv,
    acc,
    faces_out,
    faces_in,
    below,
    above,
    hout,
    weight,
    keep,
    rates_out,
    rates_in,
    wide_0,
    wide_1,
    height,
    coef,
    in_sem,
    out_sem,
    x_send,
    x_recv,
    y_send,
    y_recv,
    f_send,
    f_recv,
    a_send,
    a_recv,
    h_send,
    h_recv,
    r_send,
    r_recv,
):
    bins, species, cells, heights, radii = f_ref.shape
    total_bins = kernel_ref.shape[0]
    count = ny * nx
    wides = (wide_0, wide_1)
    phi = lax.axis_index("phi")
    mom = lax.axis_index("mom")
    phis = lax.axis_size("phi")
    row, col = mom // nx, mom % nx
    right, left = (phi + 1) % phis, (phi + phis - 1) % phis

    load = pltpu.make_async_copy(f_hbm, f_ref, in_sem)
    load.start()
    barrier = pltpu.get_barrier_semaphore()
    for d in range(1, count):
        pl.semaphore_signal(
            barrier, inc=1, device_id={"mom": (mom + d) % count}, device_id_type=MESH
        )
    for side in (left, right):
        pl.semaphore_signal(barrier, inc=1, device_id={"phi": side}, device_id_type=MESH)

    def along_row(d):
        return {"mom": row * nx + (col + d) % nx}

    def along_col(e):
        return {"mom": ((row + e) % ny) * nx + col}

    def sizes(x):
        return (nx, ny) if x % 2 == 0 else (ny, nx)

    def parent_copy(s, x, d):
        c = s * cells + x
        return pltpu.make_async_remote_copy(
            src_ref=comb.at[c, 0],
            dst_ref=comb.at[c, d],
            send_sem=x_send.at[c, d - 1],
            recv_sem=x_recv.at[c, d - 1],
            device_id=along_row(d) if x % 2 == 0 else along_col(d),
            device_id_type=MESH,
        )

    def partial_copy(s, x, e):
        c = s * cells + x
        return pltpu.make_async_remote_copy(
            src_ref=psend.at[c, e - 1],
            dst_ref=precv.at[c, e - 1],
            send_sem=y_send.at[c, e - 1],
            recv_sem=y_recv.at[c, e - 1],
            device_id=along_col(e) if x % 2 == 0 else along_row(e),
            device_id_type=MESH,
        )

    def face_copy(s, side):
        return pltpu.make_async_remote_copy(
            src_ref=faces_out.at[s, side],
            dst_ref=faces_in.at[s, side],
            send_sem=f_send.at[s, side],
            recv_sem=f_recv.at[s, side],
            device_id={"phi": left if side == 0 else right},
            device_id_type=MESH,
        )

    def below_copy(s):
        return pltpu.make_async_remote_copy(
            src_ref=below.at[s],
            dst_ref=above.at[s],
            send_sem=a_send.at[s],
            recv_sem=a_recv.at[s],
            device_id={"mom": (mom + count - 1) % count},
            device_id_type=MESH,
        )

    def h_copy(s, k):
        return pltpu.make_async_remote_copy(
            src_ref=hout.at[s],
            dst_ref=hin.at[s],
            send_sem=h_send.at[s, k],
            recv_sem=h_recv.at[s],
            device_id={"mom": (mom + count - 1 - k) % count},
            device_id_type=MESH,
        )

    def rate_copy():
        return pltpu.make_async_remote_copy(
            src_ref=rates_out,
            dst_ref=rates_in,
            send_sem=r_send,
            recv_sem=r_recv,
            device_id={"mom": (mom + count - 1) % count},
            device_id_type=MESH,
        )

    def settled_copy(s):
        part = pl.ds(s * cells, cells)
        return pltpu.make_async_copy(acc.at[part], settled_ref.at[part], out_sem.at[s])

    def fill_parents(s):
        parent = parent_ref[s]
        for x in range(cells):
            for q in range(bins):
                comb[s * cells + x, 0, q] = f_ref[q, parent, x].astype(jnp.bfloat16)

    def send_parents(s):
        for x in range(cells):
            for d in range(1, sizes(x)[0]):
                parent_copy(s, x, d).start()

    odd = mom % 2 == 1
    ahead = 2
    for p in range(bins):
        rates_out[p] = jnp.full((8, radii), rate_ref[p], jnp.float32)
    load.wait()
    fill_parents(0)
    pl.semaphore_wait(barrier, count + 1)
    send_parents(0)

    @pl.loop(1, species)
    def _(s):
        fill_parents(s)

        @pl.when(s < ahead)
        def _():
            send_parents(s)

    @pl.when(odd)
    def _():
        rate_copy().start()

    row_starts = [(row * nx + (col + d) % nx) * bins for d in range(nx)]
    col_starts = [(((row + e) % ny) * nx + col) * bins for e in range(ny)]
    row_froms = [(row * nx + (col + nx - d) % nx) * bins for d in range(nx)]
    col_froms = [(((row + ny - e) % ny) * nx + col) * bins for e in range(ny)]
    for to, source_from, ref in ((col_starts, row_froms, wide_0), (row_starts, col_froms, wide_1)):
        rows_1h = onehot_bins(to, bins, total_bins)
        cols_1h = onehot_bins(source_from, bins, total_bins)
        mixed = dot_nt(dot(rows_1h, kernel_ref[...]).astype(jnp.bfloat16), cols_1h)
        r_at = lax.broadcasted_iota(jnp.int32, mixed.shape, 0) & (ROWS - 1)
        c_at = lax.broadcasted_iota(jnp.int32, mixed.shape, 1) & (ROWS - 1)
        ref[...] = jnp.where(r_at == c_at, mixed, 0.0).astype(jnp.bfloat16)

    group = height.shape[1] // heights
    a_at = lax.broadcasted_iota(jnp.int32, (heights, heights), 0)
    b_at = lax.broadcasted_iota(jnp.int32, (heights, heights), 1)
    stencil = jnp.where(a_at == b_at, 0.5, 0.0) + jnp.where(jnp.abs(a_at - b_at) == 1, 0.25, 0.0)
    both = jnp.dot(
        inverse_ref[...],
        stencil,
        precision=lax.Precision.HIGHEST,
        preferred_element_type=jnp.float32,
    )
    high = both.astype(jnp.bfloat16).astype(jnp.float32)
    tall_a = lax.broadcasted_iota(jnp.int32, (group, heights, heights), 1)
    tall_b = lax.broadcasted_iota(jnp.int32, (group, heights, heights), 2)
    spread = jnp.where(tall_a == tall_b, 1.0, 0.0).reshape(group * heights, heights)
    spread = spread.astype(jnp.bfloat16)
    row_g = lax.broadcasted_iota(jnp.int32, (group, heights, group * heights), 0)
    col_g = lax.broadcasted_iota(jnp.int32, (group, heights, group * heights), 2)
    first = row_g * heights
    inside = jnp.where((col_g >= first) & (col_g < first + heights), 1.0, 0.0)
    inside = inside.reshape(group * heights, group * heights)
    for k, part in enumerate((high, both - high)):
        tall = jnp.concatenate([part] * group, axis=0).astype(jnp.bfloat16)
        height[k] = (dot_nt(tall, spread) * inside).astype(jnp.bfloat16)

    diff = diff_ref[...]
    lane = lax.broadcasted_iota(jnp.int32, diff.shape, 1)
    coef[0] = 1.0 - 3.0 * diff
    coef[1] = jnp.where(lane == 0, 0.0, 0.5 * diff)
    coef[2] = jnp.where(lane == radii - 1, 0.0, 0.5 * diff)

    for x in range(cells):
        kept = jnp.ones((heights, radii), jnp.float32)
        for p in range(bins):
            part = 1.0 / (1.0 + 0.5 * rate_ref[p] * density_ref[x])
            weight[p, x] = part
            kept = kept * (1.0 - part)
        keep[0, x] = kept

    def keep_above():
        rate_copy().wait_recv()
        for x in range(cells):
            kept = jnp.ones((heights // 8, 8, radii), jnp.float32)
            dens = density_ref[x].reshape(heights // 8, 8, radii)
            for p in range(bins):
                kept = kept * (1.0 - 1.0 / (1.0 + 0.5 * rates_in[p] * dens))
            keep[1, x] = kept.reshape(heights, radii)

    @pl.when(mom >= count - 2)
    def _():
        hin[...] = jnp.zeros_like(hin)

    def mix(s):
        for x in range(cells):
            c = s * cells + x
            n1, n2 = sizes(x)
            for d in range(1, n1):
                parent_copy(s, x, d).wait_recv()

            @pl.loop(0, heights // ROWS)
            def _(k):
                at = pl.ds(pl.multiple_of(k * ROWS, ROWS), ROWS)
                block = comb[c, :n1, :, at, :].reshape(n1 * bins * ROWS, radii)
                sums = dot(wides[x % 2][...], block).reshape(n2, bins, ROWS, radii)
                acc[c, :, at, :] = f_ref[:, s, x, at, :] + sums[0]
                for e in range(1, n2):
                    psend[c, e - 1, :, at, :] = sums[e].astype(jnp.bfloat16)

            for e in range(1, n2):
                partial_copy(s, x, e).start()

        @pl.when(s + ahead < species)
        def _():
            send_parents(s + ahead)

    def source(s):
        for x in range(cells):
            c = s * cells + x
            n2 = sizes(x)[1]
            for e in range(1, n2):
                partial_copy(s, x, e).wait_recv()

            @pl.loop(0, bins)
            def _(p):
                value = acc[c, p]
                for e in range(1, n2):
                    value = value + precv[c, e - 1, p].astype(jnp.float32)
                acc[c, p] = value
                rounded = value.astype(jnp.bfloat16)
                if x == 0:
                    faces_out[s, 0, p] = rounded
                if x == cells - 1:
                    faces_out[s, 1, p] = rounded

            if x == 0:
                face_copy(s, 0).start()
            if x == cells - 1:
                face_copy(s, 1).start()

    def diffuse(s):
        face_copy(s, 0).wait_recv()
        face_copy(s, 1).wait_recv()
        first = s * cells
        per = group // cells

        @pl.loop(0, bins // per)
        def _(k):
            planes = []
            for j in range(per):
                p = k * per + j
                own = [acc[first + x, p] for x in range(cells)]
                before = [faces_in[s, 1, p].astype(jnp.float32)] + own[:-1]
                after = own[1:] + [faces_in[s, 0, p].astype(jnp.float32)]
                for x in range(cells):
                    moved = coef[0] * own[x] + diff_ref[...] * (before[x] + after[x])
                    moved += coef[1] * pltpu.roll(own[x], 1, 1)
                    moved += coef[2] * pltpu.roll(own[x], radii - 1, 1)
                    planes.append(moved)
            moved = jnp.concatenate(planes, axis=0)
            high = moved.astype(jnp.bfloat16)
            low = (moved - high.astype(jnp.float32)).astype(jnp.bfloat16)
            settled = dot(height[0], high) + dot(height[0], low) + dot(height[1], high)
            for j in range(per):
                for x in range(cells):
                    n = j * cells + x
                    acc[first + x, k * per + j] = settled[n * heights : (n + 1) * heights]

        settled_copy(s).start()
        span = heights // 2
        for x in range(cells):
            @pl.loop(0, 2)
            def _(k):
                at = pl.ds(pl.multiple_of(k * span, span), span)
                carry = jnp.zeros((span, radii), jnp.float32)
                for p in range(bins - 1, -1, -1):
                    total = 2.0 * acc[first + x, p, at, :] + carry
                    carry = total - total * weight[p, x, at, :]
                below[s, x, at, :] = carry

        @pl.when(odd)
        def _():
            below_copy(s).start()

    def relay(s):
        @pl.when(odd & (mom < count - 1))
        def _():
            h_copy(s, 0).wait_recv()

        @pl.when(mom % 2 == 0)
        def _():
            @pl.when(s == 0)
            def _():
                keep_above()

            below_copy(s).wait_recv()

            @pl.when(mom < count - 2)
            def _():
                h_copy(s, 1).wait_recv()

            for x in range(cells):
                entering = above[s, x] + keep[1, x] * hin[s, x]
                hin[s, x] = entering
                hout[s, x] = below[s, x] + keep[0, x] * entering

            @pl.when(mom > 0)
            def _():
                h_copy(s, 0).start()
                h_copy(s, 1).start()

    lag = (count - 1 - mom) // 2

    @pl.loop(0, species + 3 + count // 2)
    def _(i):
        @pl.when(i < species)
        def _():
            mix(i)

        @pl.when((i >= 1) & (i < species + 1))
        def _():
            source(i - 1)

        @pl.when((i >= 2) & (i < species + 2))
        def _():
            diffuse(i - 2)

        s = i - 2 - lag

        @pl.when((s >= 0) & (s < species))
        def _():
            relay(s)

    @pl.when(odd)
    def _():
        rate_copy().wait_send()

    @pl.loop(0, species)
    def _(s):
        settled_copy(s).wait()
        for x in range(cells):
            for d in range(1, sizes(x)[0]):
                parent_copy(s, x, d).wait_send()
            for e in range(1, sizes(x)[1]):
                partial_copy(s, x, e).wait_send()
        face_copy(s, 0).wait_send()
        face_copy(s, 1).wait_send()

        @pl.when(odd)
        def _():
            below_copy(s).wait_send()

        @pl.when((mom % 2 == 0) & (mom > 0))
        def _():
            h_copy(s, 0).wait_send()
            h_copy(s, 1).wait_send()


def solve_kernel(settled_ref, hin_ref, rate_ref, density_ref, out_ref, weight):
    bins, heights, radii = weight.shape

    @pl.when(pl.program_id(1) == 0)
    def _():
        for p in range(bins):
            weight[p] = 1.0 / (1.0 + 0.5 * rate_ref[p] * density_ref[0])

    span = heights // 2

    @pl.loop(0, 2)
    def _(k):
        at = pl.ds(pl.multiple_of(k * span, span), span)
        carry = hin_ref[0, 0, at, :]
        for p in range(bins - 1, -1, -1):
            settled = settled_ref[0, p, at, :]
            total = 2.0 * settled + carry
            both = total * weight[p, at, :]
            out_ref[p, 0, 0, at, :] = both - settled
            carry = total - both


def local(
    ny,
    nx,
    spectra,
    production,
    bin_group,
    parent_of,
    diffusivity,
    height_inverse,
    loss_rate,
    density,
):
    bins, species, cells, heights, radii = spectra.shape
    same = bin_group[:, None] == bin_group[None, :]
    kernel = jnp.where(same, production, jnp.zeros_like(production))
    chunks = species * cells
    block = (bins, heights, radii)
    plane = (heights, radii)
    most = max(nx, ny)
    group = cells * max(1, 256 // (heights * cells))
    dma = pltpu.SemaphoreType.DMA
    vmem = pl.BlockSpec(memory_space=pltpu.VMEM)
    smem = pl.BlockSpec(memory_space=pltpu.SMEM)
    hbm = pl.BlockSpec(memory_space=pl.ANY)
    tall, broad = ny * bins * ROWS, nx * bins * ROWS
    settled, entering = pl.pallas_call(
        functools.partial(step_kernel, ny, nx),
        out_shape=[
            jax.ShapeDtypeStruct((chunks,) + block, jnp.float32),
            jax.ShapeDtypeStruct((species, cells) + plane, jnp.float32),
        ],
        in_specs=[hbm, vmem, smem, vmem, vmem, smem, vmem],
        out_specs=[hbm, vmem],
        scratch_shapes=[
            pltpu.VMEM(spectra.shape, jnp.float32),
            pltpu.VMEM((chunks, most) + block, jnp.bfloat16),
            pltpu.VMEM((chunks, most - 1) + block, jnp.bfloat16),
            pltpu.VMEM((chunks, most - 1) + block, jnp.bfloat16),
            pltpu.VMEM((chunks,) + block, jnp.float32),
            pltpu.VMEM((species, 2) + block, jnp.bfloat16),
            pltpu.VMEM((species, 2) + block, jnp.bfloat16),
            pltpu.VMEM((species, cells) + plane, jnp.float32),
            pltpu.VMEM((species, cells) + plane, jnp.float32),
            pltpu.VMEM((species, cells) + plane, jnp.float32),
            pltpu.VMEM((bins, cells) + plane, jnp.float32),
            pltpu.VMEM((2, cells) + plane, jnp.float32),
            pltpu.VMEM((bins, 8, radii), jnp.float32),
            pltpu.VMEM((bins, 8, radii), jnp.float32),
            pltpu.VMEM((tall, broad), jnp.bfloat16),
            pltpu.VMEM((broad, tall), jnp.bfloat16),
            pltpu.VMEM((2, group * heights, group * heights), jnp.bfloat16),
            pltpu.VMEM((3,) + plane, jnp.float32),
            dma,
            dma((species,)),
            dma((chunks, most - 1)),
            dma((chunks, most - 1)),
            dma((chunks, most - 1)),
            dma((chunks, most - 1)),
            dma((species, 2)),
            dma((species, 2)),
            dma((species,)),
            dma((species,)),
            dma((species, 2)),
            dma((species,)),
            dma,
            dma,
        ],
        compiler_params=pltpu.CompilerParams(
            collective_id=0, has_side_effects=True, vmem_limit_bytes=56 * 1024 * 1024
        ),
    )(spectra, kernel, parent_of, diffusivity, height_inverse, loss_rate, density)
    return pl.pallas_call(
        solve_kernel,
        grid=(cells, species),
        out_shape=jax.ShapeDtypeStruct(spectra.shape, jnp.float32),
        in_specs=[
            pl.BlockSpec((1,) + block, lambda x, s: (s * cells + x, 0, 0, 0)),
            pl.BlockSpec((1, 1) + plane, lambda x, s: (s, x, 0, 0)),
            smem,
            pl.BlockSpec((1,) + plane, lambda x, s: (x, 0, 0)),
        ],
        out_specs=pl.BlockSpec((bins, 1, 1) + plane, lambda x, s: (0, s, x, 0, 0)),
        scratch_shapes=[pltpu.VMEM(block, jnp.float32)],
        compiler_params=pltpu.CompilerParams(vmem_limit_bytes=60 * 1024 * 1024),
    )(settled, entering, loss_rate, density)


def solution(mesh):
    ny, nx = grid_of(mesh.shape["mom"])
    return jax.shard_map(
        functools.partial(local, ny, nx),
        mesh=mesh,
        in_specs=(
            P("mom", None, "phi", None, None),
            P(),
            P(),
            P(),
            P(),
            P(),
            P("mom"),
            P("phi", None, None),
        ),
        out_specs=P("mom", None, "phi", None, None),
        check_vma=False,
    )
```

```python
import functools
import math

import jax
import jax.numpy as jnp
from jax import lax
from jax.experimental import pallas as pl
from jax.experimental.pallas import tpu as pltpu
from jax.sharding import PartitionSpec as P

MESH = pl.DeviceIdType.MESH
ROWS = 16


def grid_of(count):
    columns = max(d for d in range(1, math.isqrt(count) + 1) if count % d == 0)
    return count // columns, columns


def dot(a, b):
    return jnp.dot(a, b, preferred_element_type=jnp.float32)


def dot_nt(a, b):
    return lax.dot_general(a, b, (((1,), (1,)), ((), ())), preferred_element_type=jnp.float32)


def onehot_bins(first_bins, bins, total):
    local = lax.broadcasted_iota(jnp.int32, (bins, ROWS, total), 0)
    whole = lax.broadcasted_iota(jnp.int32, (bins, ROWS, total), 2)
    parts = [
        jnp.where(local + first == whole, 1.0, 0.0).reshape(bins * ROWS, total)
        for first in first_bins
    ]
    return jnp.concatenate(parts, axis=0).astype(jnp.bfloat16)


def step_kernel(
    ny,
    nx,
    f_hbm,
    kernel_ref,
    parent_hbm,
    diff_hbm,
    inverse_hbm,
    rate_hbm,
    density_hbm,
    settled_ref,
    hin,
    weight,
    f_ref,
    parent_ref,
    diff_ref,
    inverse_ref,
    rate_ref,
    density_ref,
    comb,
    psend,
    precv,
    acc,
    faces_out,
    faces_in,
    below,
    above,
    hout,
    keep,
    rates_out,
    rates_in,
    wide_0,
    wide_1,
    height,
    coef,
    in_sem,
    out_sem,
    x_send,
    x_recv,
    y_send,
    y_recv,
    f_send,
    f_recv,
    a_send,
    a_recv,
    h_send,
    h_recv,
    r_send,
    r_recv,
):
    bins, species, cells, heights, radii = f_ref.shape
    total_bins = kernel_ref.shape[0]
    count = ny * nx
    wides = (wide_0, wide_1)
    phi = lax.axis_index("phi")
    mom = lax.axis_index("mom")
    phis = lax.axis_size("phi")
    row, col = mom // nx, mom % nx
    right, left = (phi + 1) % phis, (phi + phis - 1) % phis

    load = pltpu.make_async_copy(f_hbm, f_ref, in_sem.at[0])
    small = [
        pltpu.make_async_copy(parent_hbm, parent_ref, in_sem.at[1]),
        pltpu.make_async_copy(rate_hbm, rate_ref, in_sem.at[2]),
        pltpu.make_async_copy(diff_hbm, diff_ref, in_sem.at[3]),
        pltpu.make_async_copy(inverse_hbm, inverse_ref, in_sem.at[4]),
        pltpu.make_async_copy(density_hbm, density_ref, in_sem.at[5]),
    ]
    small[0].start()
    load.start()
    for copy in small[1:]:
        copy.start()
    barrier = pltpu.get_barrier_semaphore()
    for d in range(1, count):
        pl.semaphore_signal(
            barrier, inc=1, device_id={"mom": (mom + d) % count}, device_id_type=MESH
        )
    for side in (left, right):
        pl.semaphore_signal(barrier, inc=1, device_id={"phi": side}, device_id_type=MESH)

    def along_row(d):
        return {"mom": row * nx + (col + d) % nx}

    def along_col(e):
        return {"mom": ((row + e) % ny) * nx + col}

    def sizes(x):
        return (nx, ny) if x % 2 == 0 else (ny, nx)

    def parent_copy(s, x, d):
        c = s * cells + x
        return pltpu.make_async_remote_copy(
            src_ref=comb.at[c, 0],
            dst_ref=comb.at[c, d],
            send_sem=x_send.at[c, d - 1],
            recv_sem=x_recv.at[c, d - 1],
            device_id=along_row(d) if x % 2 == 0 else along_col(d),
            device_id_type=MESH,
        )

    def partial_copy(s, x, e):
        c = s * cells + x
        return pltpu.make_async_remote_copy(
            src_ref=psend.at[c, e - 1],
            dst_ref=precv.at[c, e - 1],
            send_sem=y_send.at[c, e - 1],
            recv_sem=y_recv.at[c, e - 1],
            device_id=along_col(e) if x % 2 == 0 else along_row(e),
            device_id_type=MESH,
        )

    def face_copy(s, side):
        return pltpu.make_async_remote_copy(
            src_ref=faces_out.at[s, side],
            dst_ref=faces_in.at[s, side],
            send_sem=f_send.at[s, side],
            recv_sem=f_recv.at[s, side],
            device_id={"phi": left if side == 0 else right},
            device_id_type=MESH,
        )

    def below_copy(s):
        return pltpu.make_async_remote_copy(
            src_ref=below.at[s],
            dst_ref=above.at[s],
            send_sem=a_send.at[s],
            recv_sem=a_recv.at[s],
            device_id={"mom": (mom + count - 1) % count},
            device_id_type=MESH,
        )

    def h_copy(s, k):
        return pltpu.make_async_remote_copy(
            src_ref=hout.at[s],
            dst_ref=hin.at[s],
            send_sem=h_send.at[s, k],
            recv_sem=h_recv.at[s],
            device_id={"mom": (mom + count - 1 - k) % count},
            device_id_type=MESH,
        )

    def rate_copy():
        return pltpu.make_async_remote_copy(
            src_ref=rates_out,
            dst_ref=rates_in,
            send_sem=r_send,
            recv_sem=r_recv,
            device_id={"mom": (mom + count - 1) % count},
            device_id_type=MESH,
        )

    def settled_copy(s):
        part = pl.ds(s * cells, cells)
        return pltpu.make_async_copy(acc.at[part], settled_ref.at[part], out_sem.at[s])

    def fill_parents(s):
        parent = parent_ref[s]
        for x in range(cells):
            for q in range(bins):
                comb[s * cells + x, 0, q] = f_ref[q, parent, x].astype(jnp.bfloat16)

    def send_parents(s):
        for x in range(cells):
            for d in range(1, sizes(x)[0]):
                parent_copy(s, x, d).start()

    odd = mom % 2 == 1
    ahead = 2
    small[0].wait()
    load.wait()
    fill_parents(0)
    pl.semaphore_wait(barrier, count + 1)
    send_parents(0)

    @pl.loop(1, species)
    def _(s):
        fill_parents(s)

        @pl.when(s < ahead)
        def _():
            send_parents(s)

    for copy in small[1:]:
        copy.wait()
    for p in range(bins):
        rates_out[p] = jnp.full((8, radii), rate_ref[p], jnp.float32)

    @pl.when(odd)
    def _():
        rate_copy().start()

    row_starts = [(row * nx + (col + d) % nx) * bins for d in range(nx)]
    col_starts = [(((row + e) % ny) * nx + col) * bins for e in range(ny)]
    row_froms = [(row * nx + (col + nx - d) % nx) * bins for d in range(nx)]
    col_froms = [(((row + ny - e) % ny) * nx + col) * bins for e in range(ny)]
    for to, source_from, ref in ((col_starts, row_froms, wide_0), (row_starts, col_froms, wide_1)):
        rows_1h = onehot_bins(to, bins, total_bins)
        cols_1h = onehot_bins(source_from, bins, total_bins)
        mixed = dot_nt(dot(rows_1h, kernel_ref[...]).astype(jnp.bfloat16), cols_1h)
        r_at = lax.broadcasted_iota(jnp.int32, mixed.shape, 0) & (ROWS - 1)
        c_at = lax.broadcasted_iota(jnp.int32, mixed.shape, 1) & (ROWS - 1)
        ref[...] = jnp.where(r_at == c_at, mixed, 0.0).astype(jnp.bfloat16)

    group = height.shape[1] // heights
    a_at = lax.broadcasted_iota(jnp.int32, (heights, heights), 0)
    b_at = lax.broadcasted_iota(jnp.int32, (heights, heights), 1)
    stencil = jnp.where(a_at == b_at, 0.5, 0.0) + jnp.where(jnp.abs(a_at - b_at) == 1, 0.25, 0.0)
    both = jnp.dot(
        inverse_ref[...],
        stencil,
        precision=lax.Precision.HIGHEST,
        preferred_element_type=jnp.float32,
    )
    high = both.astype(jnp.bfloat16).astype(jnp.float32)
    tall_a = lax.broadcasted_iota(jnp.int32, (group, heights, heights), 1)
    tall_b = lax.broadcasted_iota(jnp.int32, (group, heights, heights), 2)
    spread = jnp.where(tall_a == tall_b, 1.0, 0.0).reshape(group * heights, heights)
    spread = spread.astype(jnp.bfloat16)
    row_g = lax.broadcasted_iota(jnp.int32, (group, heights, group * heights), 0)
    col_g = lax.broadcasted_iota(jnp.int32, (group, heights, group * heights), 2)
    first = row_g * heights
    inside = jnp.where((col_g >= first) & (col_g < first + heights), 1.0, 0.0)
    inside = inside.reshape(group * heights, group * heights)
    for k, part in enumerate((high, both - high)):
        tall = jnp.concatenate([part] * group, axis=0).astype(jnp.bfloat16)
        height[k] = (dot_nt(tall, spread) * inside).astype(jnp.bfloat16)

    diff = diff_ref[...]
    lane = lax.broadcasted_iota(jnp.int32, diff.shape, 1)
    coef[0] = 1.0 - 3.0 * diff
    coef[1] = jnp.where(lane == 0, 0.0, 0.5 * diff)
    coef[2] = jnp.where(lane == radii - 1, 0.0, 0.5 * diff)

    for x in range(cells):
        kept = jnp.ones((heights, radii), jnp.float32)
        for p in range(bins):
            part = 1.0 / (1.0 + 0.5 * rate_ref[p] * density_ref[x])
            weight[p, x] = part
            kept = kept * (1.0 - part)
        keep[0, x] = kept

    def keep_above():
        rate_copy().wait_recv()
        for x in range(cells):
            kept = jnp.ones((heights // 8, 8, radii), jnp.float32)
            dens = density_ref[x].reshape(heights // 8, 8, radii)
            for p in range(bins):
                kept = kept * (1.0 - 1.0 / (1.0 + 0.5 * rates_in[p] * dens))
            keep[1, x] = kept.reshape(heights, radii)

    @pl.when(mom >= count - 2)
    def _():
        hin[...] = jnp.zeros_like(hin)

    def mix(s):
        for x in range(cells):
            c = s * cells + x
            n1, n2 = sizes(x)
            for d in range(1, n1):
                parent_copy(s, x, d).wait_recv()

            @pl.loop(0, heights // ROWS)
            def _(k):
                at = pl.ds(pl.multiple_of(k * ROWS, ROWS), ROWS)
                block = comb[c, :n1, :, at, :].reshape(n1 * bins * ROWS, radii)
                sums = dot(wides[x % 2][...], block).reshape(n2, bins, ROWS, radii)
                acc[c, :, at, :] = f_ref[:, s, x, at, :] + sums[0]
                for e in range(1, n2):
                    psend[c, e - 1, :, at, :] = sums[e].astype(jnp.bfloat16)

            for e in range(1, n2):
                partial_copy(s, x, e).start()

        @pl.when(s + ahead < species)
        def _():
            send_parents(s + ahead)

    def source(s):
        for x in range(cells):
            c = s * cells + x
            n2 = sizes(x)[1]
            for e in range(1, n2):
                partial_copy(s, x, e).wait_recv()

            @pl.loop(0, bins)
            def _(p):
                value = acc[c, p]
                for e in range(1, n2):
                    value = value + precv[c, e - 1, p].astype(jnp.float32)
                acc[c, p] = value
                rounded = value.astype(jnp.bfloat16)
                if x == 0:
                    faces_out[s, 0, p] = rounded
                if x == cells - 1:
                    faces_out[s, 1, p] = rounded

            if x == 0:
                face_copy(s, 0).start()
            if x == cells - 1:
                face_copy(s, 1).start()

    def diffuse(s):
        face_copy(s, 0).wait_recv()
        face_copy(s, 1).wait_recv()
        first = s * cells
        per = group // cells

        @pl.loop(0, bins // per)
        def _(k):
            planes = []
            for j in range(per):
                p = k * per + j
                own = [acc[first + x, p] for x in range(cells)]
                before = [faces_in[s, 1, p].astype(jnp.float32)] + own[:-1]
                after = own[1:] + [faces_in[s, 0, p].astype(jnp.float32)]
                for x in range(cells):
                    moved = coef[0] * own[x] + diff_ref[...] * (before[x] + after[x])
                    moved += coef[1] * pltpu.roll(own[x], 1, 1)
                    moved += coef[2] * pltpu.roll(own[x], radii - 1, 1)
                    planes.append(moved)
            moved = jnp.concatenate(planes, axis=0)
            high = moved.astype(jnp.bfloat16)
            low = (moved - high.astype(jnp.float32)).astype(jnp.bfloat16)
            settled = dot(height[0], high) + dot(height[0], low) + dot(height[1], high)
            for j in range(per):
                for x in range(cells):
                    n = j * cells + x
                    acc[first + x, k * per + j] = settled[n * heights : (n + 1) * heights]

        settled_copy(s).start()
        span = heights // 2
        for x in range(cells):
            @pl.loop(0, 2)
            def _(k):
                at = pl.ds(pl.multiple_of(k * span, span), span)
                carry = jnp.zeros((span, radii), jnp.float32)
                for p in range(bins - 1, -1, -1):
                    total = 2.0 * acc[first + x, p, at, :] + carry
                    carry = total - total * weight[p, x, at, :]
                below[s, x, at, :] = carry

    def relay(s):
        @pl.when(odd & (mom < count - 1))
        def _():
            h_copy(s, 0).wait_recv()

        @pl.when(mom % 2 == 0)
        def _():
            @pl.when(s == 0)
            def _():
                keep_above()

            below_copy(s).wait_recv()

            @pl.when(mom < count - 2)
            def _():
                h_copy(s, 1).wait_recv()

            for x in range(cells):
                entering = above[s, x] + keep[1, x] * hin[s, x]
                hin[s, x] = entering
                hout[s, x] = below[s, x] + keep[0, x] * entering

            @pl.when(mom > 0)
            def _():
                h_copy(s, 0).start()
                h_copy(s, 1).start()

    lag = (count - 1 - mom) // 2
    hold = 3

    @pl.loop(0, species + 3 + max(hold - 2, 0) + count // 2)
    def _(i):
        @pl.when(i < species)
        def _():
            mix(i)

        @pl.when((i >= 1) & (i < species + 1))
        def _():
            source(i - 1)

        @pl.when((i >= 2) & (i < species + 2))
        def _():
            diffuse(i - 2)

        for s in range(species):
            @pl.when(odd & (i == max(s + 2, hold)))
            def _():
                below_copy(s).start()

        s = i - 2 - max(hold - 2, 0) - lag

        @pl.when((s >= 0) & (s < species))
        def _():
            relay(s)

    @pl.when(odd)
    def _():
        rate_copy().wait_send()

    @pl.loop(0, species)
    def _(s):
        settled_copy(s).wait()
        for x in range(cells):
            for d in range(1, sizes(x)[0]):
                parent_copy(s, x, d).wait_send()
            for e in range(1, sizes(x)[1]):
                partial_copy(s, x, e).wait_send()
        face_copy(s, 0).wait_send()
        face_copy(s, 1).wait_send()

        @pl.when(odd)
        def _():
            below_copy(s).wait_send()

        @pl.when((mom % 2 == 0) & (mom > 0))
        def _():
            h_copy(s, 0).wait_send()
            h_copy(s, 1).wait_send()


def solve_kernel(settled_ref, hin_ref, weight_ref, out_ref):
    bins, _, heights, _ = weight_ref.shape
    span = heights // 2

    @pl.loop(0, 2)
    def _(k):
        at = pl.ds(pl.multiple_of(k * span, span), span)
        carry = hin_ref[0, 0, at, :]
        for p in range(bins - 1, -1, -1):
            settled = settled_ref[0, p, at, :]
            total = 2.0 * settled + carry
            both = total * weight_ref[p, 0, at, :]
            out_ref[p, 0, 0, at, :] = both - settled
            carry = total - both


def local(
    ny,
    nx,
    spectra,
    production,
    bin_group,
    parent_of,
    diffusivity,
    height_inverse,
    loss_rate,
    density,
):
    bins, species, cells, heights, radii = spectra.shape
    same = bin_group[:, None] == bin_group[None, :]
    kernel = jnp.where(same, production, jnp.zeros_like(production))
    chunks = species * cells
    block = (bins, heights, radii)
    plane = (heights, radii)
    most = max(nx, ny)
    group = cells * max(1, 256 // (heights * cells))
    dma = pltpu.SemaphoreType.DMA
    vmem = pl.BlockSpec(memory_space=pltpu.VMEM)
    hbm = pl.BlockSpec(memory_space=pltpu.HBM)
    free = pl.BlockSpec(memory_space=pl.ANY)
    stay = functools.partial(pltpu.with_memory_space_constraint, memory_space=pltpu.HBM)
    tall, broad = ny * bins * ROWS, nx * bins * ROWS
    settled, entering, weight = pl.pallas_call(
        functools.partial(step_kernel, ny, nx),
        out_shape=[
            jax.ShapeDtypeStruct((chunks,) + block, jnp.float32),
            jax.ShapeDtypeStruct((species, cells) + plane, jnp.float32),
            jax.ShapeDtypeStruct((bins, cells) + plane, jnp.float32),
        ],
        in_specs=[hbm, vmem, hbm, hbm, hbm, hbm, hbm],
        out_specs=[free, vmem, vmem],
        scratch_shapes=[
            pltpu.VMEM(spectra.shape, jnp.float32),
            pltpu.SMEM(parent_of.shape, jnp.int32),
            pltpu.VMEM(plane, jnp.float32),
            pltpu.VMEM(height_inverse.shape, jnp.float32),
            pltpu.SMEM(loss_rate.shape, jnp.float32),
            pltpu.VMEM(density.shape, jnp.float32),
            pltpu.VMEM((chunks, most) + block, jnp.bfloat16),
            pltpu.VMEM((chunks, most - 1) + block, jnp.bfloat16),
            pltpu.VMEM((chunks, most - 1) + block, jnp.bfloat16),
            pltpu.VMEM((chunks,) + block, jnp.float32),
            pltpu.VMEM((species, 2) + block, jnp.bfloat16),
            pltpu.VMEM((species, 2) + block, jnp.bfloat16),
            pltpu.VMEM((species, cells) + plane, jnp.float32),
            pltpu.VMEM((species, cells) + plane, jnp.float32),
            pltpu.VMEM((species, cells) + plane, jnp.float32),
            pltpu.VMEM((2, cells) + plane, jnp.float32),
            pltpu.VMEM((bins, 8, radii), jnp.float32),
            pltpu.VMEM((bins, 8, radii), jnp.float32),
            pltpu.VMEM((tall, broad), jnp.bfloat16),
            pltpu.VMEM((broad, tall), jnp.bfloat16),
            pltpu.VMEM((2, group * heights, group * heights), jnp.bfloat16),
            pltpu.VMEM((3,) + plane, jnp.float32),
            dma((6,)),
            dma((species,)),
            dma((chunks, most - 1)),
            dma((chunks, most - 1)),
            dma((chunks, most - 1)),
            dma((chunks, most - 1)),
            dma((species, 2)),
            dma((species, 2)),
            dma((species,)),
            dma((species,)),
            dma((species, 2)),
            dma((species,)),
            dma,
            dma,
        ],
        compiler_params=pltpu.CompilerParams(
            collective_id=0, has_side_effects=True, vmem_limit_bytes=28 * 1024 * 1024
        ),
    )(
        stay(spectra),
        kernel,
        stay(parent_of),
        stay(diffusivity),
        stay(height_inverse),
        stay(loss_rate),
        stay(density),
    )
    return pl.pallas_call(
        solve_kernel,
        grid=(cells, species),
        out_shape=jax.ShapeDtypeStruct(spectra.shape, jnp.float32),
        in_specs=[
            pl.BlockSpec((1,) + block, lambda x, s: (s * cells + x, 0, 0, 0)),
            pl.BlockSpec((1, 1) + plane, lambda x, s: (s, x, 0, 0)),
            pl.BlockSpec((bins, 1) + plane, lambda x, s: (0, x, 0, 0)),
        ],
        out_specs=pl.BlockSpec((bins, 1, 1) + plane, lambda x, s: (0, s, x, 0, 0)),
        compiler_params=pltpu.CompilerParams(vmem_limit_bytes=16 * 1024 * 1024),
    )(settled, entering, weight)


def solution(mesh):
    ny, nx = grid_of(mesh.shape["mom"])
    return jax.shard_map(
        functools.partial(local, ny, nx),
        mesh=mesh,
        in_specs=(
            P("mom", None, "phi", None, None),
            P(),
            P(),
            P(),
            P(),
            P(),
            P("mom"),
            P("phi", None, None),
        ),
        out_specs=P("mom", None, "phi", None, None),
        check_vma=False,
    )
```
